32 devices in a mesh: grp: 2 (over y), seq: 4 (over z), mdl: 2 (over x), pair: 2 (over core).
Axes of the slice: x: 2, y: 2, z: 4, core: 2. Of those that a mesh axis runs over, the one named last changes fastest.
Arguments:
- resp_query: bfloat16 [8192, 8192], P(('grp', 'seq', 'pair'), 'mdl'), parts along dimension 0, may hold values from -6 to 6
- resp_key: bfloat16 [8192, 1024], P(('grp', 'seq', 'pair'), 'mdl'), parts along dimension 0, may hold values from -6 to 6
- response_value: bfloat16 [8192, 1024], P(('grp', 'seq', 'pair'), 'mdl'), parts along dimension 0, may hold values from -6 to 6
- readout: bfloat16 [8192, 8192], P(('grp', 'seq', 'pair'), 'mdl'), parts along dimension 0, may hold values from -0.0625 to 0.0625
- packed_prompt_key: bfloat16 [1024, 1024], P(('grp', 'seq', 'pair'), 'mdl'), parts along dimension 0, may hold values from -6 to 6
- packed_prompt_value: bfloat16 [1024, 1024], P(('grp', 'seq', 'pair'), 'mdl'), parts along dimension 0, may hold values from -6 to 6
- prompt_owner: int32 [1024], P('grp'), parts along dimension 0, may hold values from 0 to 3, never falling along the last dimension, each value on 1 to 256 neighbouring positions
- pair_slot: int32 [8], P(('grp', 'seq')), parts along dimension 0, may hold values from 0 to 3, each once
- domain_of: int32 [8], P(('grp', 'seq')), parts along dimension 0, may hold values from 0 to 7
- resp_blocks: int32 [16], P(('grp', 'seq', 'pair')), parts along dimension 0, may hold values from 1 to 4, 20 in all
- ref_logprob: float32 [16], P(('grp', 'seq', 'pair')), parts along dimension 0, may hold values from -8 to 8
Outputs:
- grad_query: bfloat16 [8192, 8192], P(('grp', 'seq', 'pair'), 'mdl'), parts along dimension 0
- grad_resp_key: bfloat16 [8192, 1024], P(('grp', 'seq', 'pair'), 'mdl'), parts along dimension 0
- grad_resp_value: bfloat16 [8192, 1024], P(('grp', 'seq', 'pair'), 'mdl'), parts along dimension 0
- grad_prompt_key: float32 [1024, 1024], P(('grp', 'seq', 'pair'), 'mdl'), parts along dimension 0
- grad_prompt_value: float32 [1024, 1024], P(('grp', 'seq', 'pair'), 'mdl'), parts along dimension 0
The draws below stay inside these ranges and needn't reach their ends.
There are 2 independent parts, one for each index of `grp`. The reference program is written for one: setup_inputs(seed, part) draws one part's arguments, and reference() takes and returns one part's arrays. A program takes and returns all parts, laid end to end along the dimension named above; each array names one. Nothing has to cross between parts.
Inputs may be any that keep to these rules, and one draw needn't show every extreme that they name: `prompt_owner`: ids never fall along the prompt; every one of the 4 pairs owns at least one prompt token and the longest prompt has exactly 256 tokens. `pair_slot`: each pair is held at exactly one index. `resp_blocks`: some response fills all 4 blocks.
All inputs are finite; a program needn't handle non-finite values.
Results may differ from the reference program's by a relative error of at most 0.015.
Values may be sent and summed in bfloat16 or wider, within the bound.
A program may use at most 128 MiB of HBM per device.

```python
import math
import jax
import jax.numpy as jnp
import numpy as np
from jax import lax

QUERY_HEAD_COUNT = 64
KEY_VALUE_HEADS = 8
HEAD_SIZE = 128
RESP_DEV = 512
PROMPT_DEV = 64
BLK = 128
NDOM = 8
RESP_BLK = 4
RESPONSE_ROWS = 4096
PROMPT_TOKENS = 512
N_SEQ = 4


def draw_resp_query(key, part):
    key = jax.random.fold_in(key, 1)
    value_arrays = jnp.clip(jax.random.normal(key, (RESPONSE_ROWS, QUERY_HEAD_COUNT * HEAD_SIZE), jnp.float32), -4.0, 4.0)
    return value_arrays.astype(jnp.bfloat16)


def draw_resp_key(key, part):
    key = jax.random.fold_in(key, 2)
    value_arrays = jnp.clip(jax.random.normal(key, (RESPONSE_ROWS, KEY_VALUE_HEADS * HEAD_SIZE), jnp.float32), -4.0, 4.0)
    return value_arrays.astype(jnp.bfloat16)


def plant(drawn, own_key, least, high):
    longest = drawn.shape.index(max(drawn.shape))
    spots = []
    for shift in (0, 1):
        where = [jax.random.randint(jax.random.fold_in(own_key, axis), (), 0, length) for axis, length in enumerate(drawn.shape)]
        where[longest] = (where[longest] + shift) % drawn.shape[longest]
        spots.append(tuple(where))
    return drawn.at[spots[0]].set(least).at[spots[1]].set(high)


def levels(stream_key, dims, split, least, top_value):
    gain = 1.0
    for position, blocks in split:
        draws = jax.random.uniform(jax.random.fold_in(jax.random.fold_in(stream_key, 6), position), (blocks,), jnp.float32, least / len(split), top_value / len(split))
        gain = gain * jnp.repeat(jnp.exp(draws), dims[position] // blocks).reshape((-1,) + (1,) * (len(dims) - 1 - position))
    return gain


def rank_bounds(count, skew):
    portions = [(1 << 20) // math.isqrt(rank ** skew) + 1 for rank in range(1, count + 1)]
    deviation = 1 + sum(portions) // (1 << 30)
    return np.cumsum(np.array([max(1, weight // deviation) for weight in portions]))


def ranked_ids(stream_key, extent, count, lean):
    grid = rank_bounds(count, lean)
    lot = jax.random.randint(jax.random.fold_in(stream_key, 1), extent, 0, int(grid[count - 1]))
    standing = jnp.searchsorted(jnp.asarray(grid, jnp.int32), lot, side="right")
    return jax.random.permutation(jax.random.fold_in(stream_key, 2), count)[standing].astype(jnp.int32)


def profile(amount, total, limit, skew):
    loads = [(1 << 20) // math.isqrt(grade ** skew) + 1 for grade in range(2, amount + 1)]
    spare, given = total - limit - (amount - 1), [1] * (amount - 1)
    while spare > 0:
        candidates = [i for i in range(amount - 1) if given[i] < limit]
        pool, remaining = sum([loads[i] for i in candidates]), spare
        for i in candidates:
            more = min(limit - given[i], max(1, remaining * loads[i] // pool), spare)
            given[i] = given[i] + more
            spare = spare - more
    return np.array([limit] + given)


def ragged_sizes(key, number_of, total, limit, skew):
    if number_of == 2:
        one = jax.random.randint(key, (), max(1, total - limit), min(limit, total - 1) + 1)
        return jnp.stack([one, total - one])
    lengths = jnp.asarray(profile(number_of, total, limit, skew), jnp.int32)
    couples = (number_of - 1) // 2
    source_of, receiver = lengths[1:1 + 2 * couples:2], lengths[2:2 + 2 * couples:2]
    room = jnp.minimum(source_of - 1, limit - receiver)
    shifted = jax.random.randint(jax.random.fold_in(key, 1), (couples,), 0, 1 << 20) % (room + 1)
    lengths = lengths.at[1:1 + 2 * couples:2].set(source_of - shifted).at[2:2 + 2 * couples:2].set(receiver + shifted)
    return lengths[jax.random.permutation(jax.random.fold_in(key, 2), number_of)]


def noise(own_key, extent, spread, reach, split=(), kind=jnp.bfloat16):
    array = jax.random.normal(own_key, extent, jnp.float32) * spread
    if len(split) > 0:
        array = levels(own_key, extent, split, -0.22, 0.18) * array
    return jnp.clip(array, min=-reach, max=reach).astype(kind)


def setup_inputs(seed: int = 0, part: int = 0) -> dict:
    keys = jax.random.split(jax.random.key(seed), 12)
    part_keys = jax.random.split(jax.random.fold_in(keys[11], part), 12)
    return {
        "resp_query": draw_resp_query(jax.random.fold_in(jax.random.fold_in(keys[11], part), 71), part),
        "resp_key": draw_resp_key(jax.random.fold_in(jax.random.fold_in(keys[11], part), 71), part),
        "response_value": noise(part_keys[2], (RESPONSE_ROWS, KEY_VALUE_HEADS * HEAD_SIZE), 1.0, 6.0, ((0, 8), (1, 2))),
        "readout": noise(part_keys[3], (RESPONSE_ROWS, QUERY_HEAD_COUNT * HEAD_SIZE), (QUERY_HEAD_COUNT * HEAD_SIZE) ** -0.5, 0.0625, ((0, 8), (1, 2))),
        "packed_prompt_key": noise(part_keys[4], (PROMPT_TOKENS, KEY_VALUE_HEADS * HEAD_SIZE), 1.0, 6.0, ((0, 8), (1, 2))),
        "packed_prompt_value": noise(part_keys[5], (PROMPT_TOKENS, KEY_VALUE_HEADS * HEAD_SIZE), 1.0, 6.0, ((0, 8), (1, 2))),
        "prompt_owner": jnp.searchsorted(jnp.cumsum(ragged_sizes(part_keys[6], N_SEQ, PROMPT_TOKENS, 4 * PROMPT_DEV, 2)), jnp.arange(PROMPT_TOKENS), side="right").astype(jnp.int32),
        "pair_slot": jax.random.permutation(part_keys[7], N_SEQ).astype(jnp.int32),
        "domain_of": plant(ranked_ids(part_keys[8], (N_SEQ,), NDOM, 2), jax.random.fold_in(part_keys[8], 3), 0, NDOM - 1).astype(jnp.int32),
        "resp_blocks": ragged_sizes(part_keys[9], 2 * N_SEQ, 5 * N_SEQ * RESP_BLK // 4, RESP_BLK, 2).astype(jnp.int32),
        "ref_logprob": noise(part_keys[10], (2 * N_SEQ,), 2.0, 8.0, ((0, 8),), jnp.float32),
    }


dpo_beta = 0.5
loss_scale = 256.0


def product(form, left, right):
    return jnp.einsum(form, left.astype(jnp.float32), right.astype(jnp.float32), precision=lax.Precision.HIGHEST)


def by_head(value_arrays, key_value_heads):
    return jnp.moveaxis(value_arrays.reshape(value_arrays.shape[0], key_value_heads, -1, HEAD_SIZE), 1, 0)


def kv_by_head(value_arrays, key_value_heads):
    return jnp.moveaxis(value_arrays.reshape(value_arrays.shape[0], key_value_heads, HEAD_SIZE), 1, 0)


def merge_heads(value_arrays):
    return jnp.moveaxis(value_arrays, 0, 1).reshape(value_arrays.shape[1], -1)


def visibility(prompt_visible, row_count):
    order = jnp.arange(row_count)
    causal = order[None, :] <= order[:, None]
    prompt_wide = jnp.broadcast_to(prompt_visible[None, :], (row_count, prompt_visible.shape[0]))
    return prompt_wide, causal


def head_forward(queries, key_rows, value_rows, visible):
    scores = product("rgd,kd->grk", queries, key_rows) * (queries.shape[-1] ** -0.5)
    scores = jnp.where(visible[None], scores, -jnp.inf)
    row_max = jnp.max(scores, axis=-1, keepdims=True)
    exponent = jnp.exp(scores - row_max)
    row_sum = jnp.sum(exponent, axis=-1, keepdims=True)
    weights = (exponent / row_sum).astype(jnp.bfloat16)
    outputs = product("grk,kd->rgd", weights, value_rows)
    return outputs, row_max + jnp.log(row_sum)


def head_backward(queries, key_rows, value_rows, visible, log_norm, grad_half, grad_row):
    scale_factor = queries.shape[-1] ** -0.5
    scores = product("rgd,kd->grk", queries, key_rows) * scale_factor
    weights = jnp.where(visible[None], jnp.exp(scores - log_norm), 0.0)
    weight_half = weights.astype(jnp.bfloat16)
    grad_value = product("grk,rgd->kd", weight_half, grad_half)
    grad_prob = product("rgd,kd->grk", grad_half, value_rows)
    grad_score = (weights * (grad_prob - grad_row)).astype(jnp.bfloat16)
    grad_query = product("grk,kd->rgd", grad_score, key_rows) * scale_factor
    grad_key = product("grk,rgd->kd", grad_score, queries) * scale_factor
    return grad_query, grad_key, grad_value


def sequence_forward(queries, resp_key, response_value, packed_prompt_key, packed_prompt_value, prompt_visible):
    key_value_heads = resp_key.shape[1] // HEAD_SIZE
    prompt_wide, causal = visibility(prompt_visible, queries.shape[0])
    visible = jnp.concatenate([prompt_wide, causal], axis=1)
    key_all = kv_by_head(jnp.concatenate([packed_prompt_key, resp_key], axis=0), key_value_heads)
    value_all = kv_by_head(jnp.concatenate([packed_prompt_value, response_value], axis=0), key_value_heads)
    return lax.map(lambda operands: head_forward(operands[0], operands[1], operands[2], visible), (by_head(queries, key_value_heads), key_all, value_all))


def sequence_backward(queries, resp_key, response_value, packed_prompt_key, packed_prompt_value, prompt_visible, log_norm, grad_half, grad_row):
    key_value_heads = resp_key.shape[1] // HEAD_SIZE
    prompt_wide, causal = visibility(prompt_visible, queries.shape[0])

    def per_head(operands):
        query_prompt, key_prompt, value_prompt = head_backward(operands[0], operands[1], operands[2], prompt_wide, operands[5], operands[6], operands[7])
        query_self, key_self, value_self = head_backward(operands[0], operands[3], operands[4], causal, operands[5], operands[6], operands[7])
        return query_prompt + query_self, key_prompt, value_prompt, key_self, value_self

    results = lax.map(per_head, (by_head(queries, key_value_heads), kv_by_head(packed_prompt_key, key_value_heads), kv_by_head(packed_prompt_value, key_value_heads), kv_by_head(resp_key, key_value_heads), kv_by_head(response_value, key_value_heads), log_norm, grad_half, grad_row))
    return merge_heads(results[0]), merge_heads(results[1]), merge_heads(results[2]), merge_heads(results[3]), merge_heads(results[4])


def reference(resp_query, resp_key, response_value, readout, packed_prompt_key, packed_prompt_value, prompt_owner, pair_slot, domain_of, resp_blocks, ref_logprob):
    key_value_heads = KEY_VALUE_HEADS
    block_count = 2 * N_SEQ

    def forward_block(index):
        start = index * RESP_DEV
        taken = [lax.dynamic_slice_in_dim(source, start, RESP_DEV, 0) for source in (resp_query, resp_key, response_value, readout)]
        prompt_visible = prompt_owner == pair_slot[index // 2]
        token_valid = jnp.arange(RESP_DEV) < resp_blocks[index] * BLK
        outputs, log_norm = sequence_forward(taken[0], taken[1], taken[2], packed_prompt_key, packed_prompt_value, prompt_visible)
        read_heads = by_head(taken[3], key_value_heads)
        partial_sum = jnp.sum(jnp.where(token_valid[None, :, None, None], outputs * read_heads.astype(jnp.float32), 0.0))
        return taken, prompt_visible, token_valid, outputs, log_norm, partial_sum

    indices = jnp.arange(block_count, dtype=jnp.int32)
    logprob = lax.map(lambda index: forward_block(index)[5], indices)
    gaps = logprob - ref_logprob
    margin = dpo_beta * (gaps[0::2] - gaps[1::2])
    domain_slots = jnp.arange(NDOM)
    matches = domain_of[:, None] == domain_slots[None, :]
    counts = jnp.sum(jnp.where(matches, 1.0, 0.0), axis=0)
    own_count = jnp.sum(jnp.where(matches, counts[None, :], 0.0), axis=1)
    weight = N_SEQ / (NDOM * own_count)
    coef_chosen = -loss_scale * weight * dpo_beta * jax.nn.sigmoid(-margin)
    coefs = jnp.stack([coef_chosen, -coef_chosen], axis=1).reshape(block_count)

    def backward_block(carry, index):
        taken, prompt_visible, token_valid, outputs, log_norm, unused_sum = forward_block(index)
        grad_full = jnp.where(token_valid[:, None], coefs[index] * taken[3].astype(jnp.float32), 0.0)
        grad_heads = by_head(grad_full, key_value_heads)
        grad_row = jnp.moveaxis(jnp.sum(grad_heads * outputs, axis=-1), 1, 2)[..., None]
        grad_half = grad_heads.astype(jnp.bfloat16)
        results = sequence_backward(taken[0], taken[1], taken[2], packed_prompt_key, packed_prompt_value, prompt_visible, log_norm, grad_half, grad_row)
        carry = (carry[0] + results[1], carry[1] + results[2])
        return carry, (results[0].astype(jnp.bfloat16), results[3].astype(jnp.bfloat16), results[4].astype(jnp.bfloat16))

    zero_grad = jnp.zeros(packed_prompt_key.shape, jnp.float32)
    prompt_grads, stacked = lax.scan(backward_block, (zero_grad, zero_grad), indices)
    grad_query = stacked[0].reshape(block_count * RESP_DEV, -1)
    grad_resp_key = stacked[1].reshape(block_count * RESP_DEV, -1)
    grad_resp_value = stacked[2].reshape(block_count * RESP_DEV, -1)
    return grad_query, grad_resp_key, grad_resp_value, prompt_grads[0], prompt_grads[1]
```

```python
import functools
import math

import jax
import jax.numpy as jnp
from jax import lax
from jax.experimental import pallas as pl
from jax.experimental.pallas import tpu as pltpu
from jax.sharding import PartitionSpec as P

HEAD_SIZE = 128
PROMPT_DEV = 64
BLK = 128
NDOM = 8
WINDOW = 4 * PROMPT_DEV
NEG = -1e30

dpo_beta = 0.5
loss_scale = 256.0


def dot(left, right, left_dim, right_dim):
    return lax.dot_general(
        left, right, (((left_dim,), (right_dim,)), ((), ())), preferred_element_type=jnp.float32
    )


def head_chain(rb, heads, q_ref, r_ref, dq_ref, lp_ref, kcat, vcat, kt, bias, tri, dkacc, dvacc):
    scale = HEAD_SIZE**-0.5
    log_scale = scale * math.log2(math.e)
    seen = WINDOW + BLK * (rb + 1)
    rows = slice(rb * BLK, (rb + 1) * BLK)
    queries = jnp.concatenate([q_ref[rows, h * HEAD_SIZE : (h + 1) * HEAD_SIZE] for h in heads], axis=0)
    reads = jnp.concatenate([r_ref[rows, h * HEAD_SIZE : (h + 1) * HEAD_SIZE] for h in heads], axis=0)
    scores = dot(kcat[:seen, :], queries, 1, 1)
    dprob = dot(vcat[:seen, :], reads, 1, 1)
    wide = len(heads)
    prompt_bias = jnp.concatenate([bias[...]] * wide, axis=1)
    diagonal = jnp.concatenate([tri[...]] * wide, axis=1)
    parts = [scores[:WINDOW] + prompt_bias]
    if rb:
        parts.append(scores[WINDOW : seen - BLK])
    parts.append(scores[seen - BLK :] + diagonal)
    scores = jnp.concatenate(parts, axis=0)
    top = jnp.max(scores, axis=0, keepdims=True) * log_scale
    exponent = jnp.exp2(scores * log_scale - top)
    inverse = 1.0 / jnp.sum(exponent, axis=0, keepdims=True)
    row_dot = jnp.sum(exponent * dprob, axis=0, keepdims=True) * inverse
    weights = exponent * inverse
    dscore = (weights * (dprob - row_dot)).astype(jnp.bfloat16)
    weights = weights.astype(jnp.bfloat16)
    dvacc[:seen, :] += dot(weights, reads, 1, 0)
    dkacc[:seen, :] += dot(dscore, queries, 1, 0)
    dq = (dot(kt[:, :seen], dscore, 1, 0) * scale).T.astype(jnp.bfloat16)
    for n, h in enumerate(heads):
        dq_ref[rows, h * HEAD_SIZE : (h + 1) * HEAD_SIZE] = dq[n * BLK : (n + 1) * BLK]
        lp_ref[0:1, :] += row_dot[:, n * BLK : (n + 1) * BLK]


def attention_kernel(
    group, at_once, blocks_ref, slot_ref, owner_ref, q_ref, r_ref, k_ref, v_ref, gk_ref, gv_ref,
    dq_ref, dk_ref, dv_ref, pk_ref, pv_ref, lp_ref,
    sel, bias, tri, kcat, vcat, kt, dkacc, dvacc,
):
    @pl.when(pl.program_id(0) == 0)
    def _():
        owner = owner_ref[...]
        slot = slot_ref[0]
        first = jnp.sum(jnp.where(owner < slot, 1.0, 0.0), axis=1, keepdims=True).astype(jnp.int32)
        column = lax.broadcasted_iota(jnp.int32, sel.shape, 1)
        row = lax.broadcasted_iota(jnp.int32, sel.shape, 0)
        chosen = jnp.where((column - row == first) & (owner == slot), 1.0, 0.0)
        sel[...] = chosen.astype(jnp.bfloat16)
        shown = jnp.sum(chosen, axis=1, keepdims=True)
        bias[...] = jnp.broadcast_to(jnp.where(shown > 0.5, 0.0, NEG), bias.shape)
        key = lax.broadcasted_iota(jnp.int32, tri.shape, 0)
        query = lax.broadcasted_iota(jnp.int32, tri.shape, 1)
        tri[...] = jnp.where(key > query, NEG, 0.0)
        lp_ref[...] = jnp.zeros_like(lp_ref)

    kcat[:WINDOW, :] = dot(sel[...], gk_ref[...], 1, 0).astype(jnp.bfloat16)
    vcat[:WINDOW, :] = dot(sel[...], gv_ref[...], 1, 0).astype(jnp.bfloat16)
    kcat[WINDOW:, :] = k_ref[...]
    vcat[WINDOW:, :] = v_ref[...]
    kt[...] = kcat[...].T
    dkacc[...] = jnp.zeros_like(dkacc)
    dvacc[...] = jnp.zeros_like(dvacc)
    for rb in range(q_ref.shape[0] // BLK):

        @pl.when(rb < blocks_ref[0])
        def _():
            for start in range(0, group, at_once):
                head_chain(
                    rb, list(range(start, start + at_once)), q_ref, r_ref, dq_ref, lp_ref,
                    kcat, vcat, kt, bias, tri, dkacc, dvacc,
                )

        @pl.when(rb >= blocks_ref[0])
        def _():
            dq_ref[rb * BLK : (rb + 1) * BLK, :] = jnp.zeros((BLK, dq_ref.shape[1]), dq_ref.dtype)

    scale = HEAD_SIZE**-0.5
    dk_ref[...] = (dkacc[WINDOW:, :] * scale).astype(dk_ref.dtype)
    dv_ref[...] = dvacc[WINDOW:, :].astype(dv_ref.dtype)
    pk_ref[...] = dot(sel[...], (dkacc[:WINDOW, :] * scale).astype(jnp.bfloat16), 0, 0).astype(pk_ref.dtype)
    pv_ref[...] = dot(sel[...], dvacc[:WINDOW, :].astype(jnp.bfloat16), 0, 0).astype(pv_ref.dtype)


def attention(q, r, k, v, gk, gv, owner, slot, blocks):
    rows, columns = q.shape
    tokens = gk.shape[0]
    heads = k.shape[1] // HEAD_SIZE
    group = columns // k.shape[1]
    wide = pl.BlockSpec((rows, group * HEAD_SIZE), lambda g: (0, g))
    slim = pl.BlockSpec((rows, HEAD_SIZE), lambda g: (0, g))
    packed = pl.BlockSpec((tokens, HEAD_SIZE), lambda g: (0, g))
    smem = pl.BlockSpec(memory_space=pltpu.SMEM)
    keys = WINDOW + rows
    bf16, f32 = jnp.bfloat16, jnp.float32
    return pl.pallas_call(
        functools.partial(attention_kernel, group, 2),
        grid=(heads,),
        in_specs=[smem, smem, pl.BlockSpec((1, tokens), lambda g: (0, 0)), wide, wide, slim, slim, packed, packed],
        out_specs=[wide, slim, slim, packed, packed, pl.BlockSpec((8, BLK), lambda g: (0, 0))],
        out_shape=[
            jax.ShapeDtypeStruct((rows, columns), bf16),
            jax.ShapeDtypeStruct(k.shape, bf16),
            jax.ShapeDtypeStruct(k.shape, bf16),
            jax.ShapeDtypeStruct(gk.shape, bf16),
            jax.ShapeDtypeStruct(gk.shape, bf16),
            jax.ShapeDtypeStruct((8, BLK), f32),
        ],
        scratch_shapes=[
            pltpu.VMEM((WINDOW, tokens), bf16),
            pltpu.VMEM((WINDOW, HEAD_SIZE), f32),
            pltpu.VMEM((BLK, BLK), f32),
            pltpu.VMEM((keys, HEAD_SIZE), bf16),
            pltpu.VMEM((keys, HEAD_SIZE), bf16),
            pltpu.VMEM((HEAD_SIZE, keys), bf16),
            pltpu.VMEM((keys, HEAD_SIZE), f32),
            pltpu.VMEM((keys, HEAD_SIZE), f32),
        ],
        compiler_params=pltpu.CompilerParams(vmem_limit_bytes=48 * 1024 * 1024),
        cost_estimate=pl.CostEstimate(flops=12 * 10**9, bytes_accessed=16 * 2**20, transcendentals=10**7),
        name="attention_gradients",
    )(blocks, slot, owner, q, r, k, v, gk, gv)


def per_device(
    resp_query, resp_key, response_value, readout, packed_prompt_key, packed_prompt_value,
    prompt_owner, pair_slot, domain_of, resp_blocks, ref_logprob,
):
    seq_count = lax.axis_size("seq")
    width = packed_prompt_key.shape[1]
    packed = jnp.concatenate([packed_prompt_key, packed_prompt_value], axis=1)
    gathered = lax.all_gather(packed, ("seq", "pair"), axis=0, tiled=True)
    dq, dk, dv, pk, pv, lp = attention(
        resp_query, readout, resp_key, response_value, gathered[:, :width], gathered[:, width:],
        prompt_owner[None, :], pair_slot, resp_blocks,
    )
    side = lax.axis_index("pair")
    domain_slots = jnp.arange(NDOM)
    counts = lax.psum(jnp.where(domain_slots == domain_of[0], 1.0, 0.0).astype(jnp.float32), "seq")
    own_gap = lax.psum(jnp.sum(lp[0]), "mdl") - ref_logprob[0]
    other_gap = lax.ppermute(own_gap, "pair", [(0, 1), (1, 0)])
    sign = jnp.where(side == 0, 1.0, -1.0)
    margin = dpo_beta * sign * (own_gap - other_gap)
    own_count = jnp.sum(jnp.where(domain_slots == domain_of[0], counts, 0.0))
    weight = seq_count / (NDOM * own_count)
    coef = -sign * loss_scale * weight * dpo_beta * jax.nn.sigmoid(-margin)
    placed = (jnp.concatenate([pk, pv], axis=1).astype(jnp.float32) * coef).astype(jnp.bfloat16)
    summed = lax.psum_scatter(placed, ("seq", "pair"), scatter_dimension=0, tiled=True).astype(jnp.float32)

    def scaled(array):
        return (array.astype(jnp.float32) * coef).astype(jnp.bfloat16)

    return scaled(dq), scaled(dk), scaled(dv), summed[:, :width], summed[:, width:]


def solution(mesh):
    tokens = P(("grp", "seq", "pair"), "mdl")
    each = P(("grp", "seq", "pair"))
    in_specs = (tokens,) * 6 + (P("grp"), P(("grp", "seq")), P(("grp", "seq")), each, each)
    return jax.shard_map(per_device, mesh=mesh, in_specs=in_specs, out_specs=(tokens,) * 5, check_vma=False)
```

```python
import functools
import math

import jax
import jax.numpy as jnp
from jax import lax
from jax.experimental import pallas as pl
from jax.experimental.pallas import tpu as pltpu
from jax.sharding import PartitionSpec as P

HEAD_SIZE = 128
PROMPT_DEV = 64
BLK = 128
NDOM = 8
WINDOW = 4 * PROMPT_DEV
NEG = -1e30
AT_ONCE = 2

dpo_beta = 0.5
loss_scale = 256.0


def dot(left, right, left_dim, right_dim):
    return lax.dot_general(
        left, right, (((left_dim,), (right_dim,)), ((), ())), preferred_element_type=jnp.float32
    )


def open_chain(rb, heads, q_ref, r_ref, kcat, vcat):
    seen = WINDOW + BLK * (rb + 1)
    rows = slice(rb * BLK, (rb + 1) * BLK)
    queries = jnp.concatenate([q_ref[rows, h * HEAD_SIZE : (h + 1) * HEAD_SIZE] for h in heads], axis=0)
    reads = jnp.concatenate([r_ref[rows, h * HEAD_SIZE : (h + 1) * HEAD_SIZE] for h in heads], axis=0)
    return queries, reads, dot(kcat[:seen, :], queries, 1, 1), dot(vcat[:seen, :], reads, 1, 1)


def weigh_chain(rb, heads, state, blocks, bias, tri):
    queries, reads, scores, dprob = state
    log_scale = HEAD_SIZE**-0.5 * math.log2(math.e)
    seen = WINDOW + BLK * (rb + 1)
    wide = len(heads)
    parts = [scores[:WINDOW] + jnp.concatenate([bias[...]] * wide, axis=1)]
    if rb:
        parts.append(scores[WINDOW : seen - BLK])
    parts.append(scores[seen - BLK :] + jnp.concatenate([tri[...]] * wide, axis=1))
    scores = jnp.concatenate(parts, axis=0)
    top = jnp.max(scores, axis=0, keepdims=True) * log_scale
    exponent = jnp.exp2(scores * log_scale - top)
    inverse = jnp.where(rb < blocks, 1.0, 0.0) / jnp.sum(exponent, axis=0, keepdims=True)
    row_dot = jnp.sum(exponent * dprob, axis=0, keepdims=True) * inverse
    weights = exponent * inverse
    dscore = (weights * (dprob - row_dot)).astype(jnp.bfloat16)
    return queries, reads, weights.astype(jnp.bfloat16), dscore, row_dot


def close_chain(rb, heads, state, dq_ref, lp_ref, kt, dkacc, dvacc):
    queries, reads, weights, dscore, row_dot = state
    seen = WINDOW + BLK * (rb + 1)
    rows = slice(rb * BLK, (rb + 1) * BLK)
    dvacc[:seen, :] += dot(weights, reads, 1, 0)
    dkacc[:seen, :] += dot(dscore, queries, 1, 0)
    dq = (dot(kt[:, :seen], dscore, 1, 0) * HEAD_SIZE**-0.5).T.astype(jnp.bfloat16)
    for n, h in enumerate(heads):
        dq_ref[rows, h * HEAD_SIZE : (h + 1) * HEAD_SIZE] = dq[n * BLK : (n + 1) * BLK]
        lp_ref[0:1, :] += row_dot[:, n * BLK : (n + 1) * BLK]


def run_chains(chains, blocks, q_ref, r_ref, dq_ref, lp_ref, kcat, vcat, kt, bias, tri, dkacc, dvacc):
    opened = open_chain(*chains[0], q_ref, r_ref, kcat, vcat)
    weighed = None
    for n, chain in enumerate(chains):
        following = open_chain(*chains[n + 1], q_ref, r_ref, kcat, vcat) if n + 1 < len(chains) else None
        done = weigh_chain(*chain, opened, blocks, bias, tri)
        if weighed is not None:
            close_chain(*chains[n - 1], weighed, dq_ref, lp_ref, kt, dkacc, dvacc)
        opened, weighed = following, done
    close_chain(*chains[-1], weighed, dq_ref, lp_ref, kt, dkacc, dvacc)


def attention_kernel(
    group, at_once, blocks_ref, slot_ref, domain_ref, ref_ref, owner_ref, q_ref, r_ref, k_ref, v_ref, gk_ref, gv_ref,
    dq_ref, dk_ref, dv_ref, pk_ref, pv_ref, lp_ref,
    sel, bias, tri, kcat, vcat, kt, dkacc, dvacc,
):
    @pl.when(pl.program_id(0) == 0)
    def _():
        owner = owner_ref[...]
        slot = slot_ref[0]
        first = jnp.sum(jnp.where(owner < slot, 1.0, 0.0), axis=1, keepdims=True).astype(jnp.int32)
        column = lax.broadcasted_iota(jnp.int32, sel.shape, 1)
        row = lax.broadcasted_iota(jnp.int32, sel.shape, 0)
        chosen = jnp.where((column - row == first) & (owner == slot), 1.0, 0.0)
        sel[...] = chosen.astype(jnp.bfloat16)
        shown = jnp.sum(chosen, axis=1, keepdims=True)
        bias[...] = jnp.broadcast_to(jnp.where(shown > 0.5, 0.0, NEG), bias.shape)
        key = lax.broadcasted_iota(jnp.int32, tri.shape, 0)
        query = lax.broadcasted_iota(jnp.int32, tri.shape, 1)
        tri[...] = jnp.where(key > query, NEG, 0.0)
        line = lax.broadcasted_iota(jnp.int32, lp_ref.shape, 0)
        domain = jnp.full(lp_ref.shape, domain_ref[0], jnp.int32).astype(jnp.float32)
        lp_ref[...] = jnp.where(line == 1, ref_ref[0], jnp.where(line == 2, domain, 0.0))

    kcat[:WINDOW, :] = dot(sel[...], gk_ref[...], 1, 0).astype(jnp.bfloat16)
    vcat[:WINDOW, :] = dot(sel[...], gv_ref[...], 1, 0).astype(jnp.bfloat16)
    kcat[WINDOW:, :] = k_ref[...]
    vcat[WINDOW:, :] = v_ref[...]
    kt[...] = kcat[...].T
    dkacc[...] = jnp.zeros_like(dkacc)
    dvacc[...] = jnp.zeros_like(dvacc)
    chains = [(rb, tuple(range(start, start + at_once))) for rb in range(q_ref.shape[0] // BLK) for start in range(0, group, at_once)]
    run_chains(chains, blocks_ref[0], q_ref, r_ref, dq_ref, lp_ref, kcat, vcat, kt, bias, tri, dkacc, dvacc)
    scale = HEAD_SIZE**-0.5
    dk_ref[...] = (dkacc[WINDOW:, :] * scale).astype(dk_ref.dtype)
    dv_ref[...] = dvacc[WINDOW:, :].astype(dv_ref.dtype)
    pk_ref[...] = dot(sel[...], (dkacc[:WINDOW, :] * scale).astype(jnp.bfloat16), 0, 0).astype(pk_ref.dtype)
    pv_ref[...] = dot(sel[...], dvacc[:WINDOW, :].astype(jnp.bfloat16), 0, 0).astype(pv_ref.dtype)


def attention(q, r, k, v, packed_kv, owner, slot, blocks, domain, ref):
    rows, columns = q.shape
    tokens = packed_kv.shape[0]
    heads = k.shape[1] // HEAD_SIZE
    group = columns // k.shape[1]
    wide = pl.BlockSpec((rows, group * HEAD_SIZE), lambda g: (0, g))
    slim = pl.BlockSpec((rows, HEAD_SIZE), lambda g: (0, g))
    packed = pl.BlockSpec((tokens, HEAD_SIZE), lambda g: (0, g))
    packed_value = pl.BlockSpec((tokens, HEAD_SIZE), lambda g: (0, heads + g))
    smem = pl.BlockSpec(memory_space=pltpu.SMEM)
    keys = WINDOW + rows
    bf16, f32 = jnp.bfloat16, jnp.float32
    return pl.pallas_call(
        functools.partial(attention_kernel, group, AT_ONCE),
        grid=(heads,),
        in_specs=[smem] * 4
        + [pl.BlockSpec((1, tokens), lambda g: (0, 0)), wide, wide, slim, slim, packed, packed_value],
        out_specs=[wide, slim, slim, packed, packed, pl.BlockSpec((8, BLK), lambda g: (0, 0))],
        out_shape=[
            jax.ShapeDtypeStruct((rows, columns), bf16),
            jax.ShapeDtypeStruct(k.shape, bf16),
            jax.ShapeDtypeStruct(k.shape, bf16),
            jax.ShapeDtypeStruct((tokens, k.shape[1]), bf16),
            jax.ShapeDtypeStruct((tokens, k.shape[1]), bf16),
            jax.ShapeDtypeStruct((8, BLK), f32),
        ],
        scratch_shapes=[
            pltpu.VMEM((WINDOW, tokens), bf16),
            pltpu.VMEM((WINDOW, HEAD_SIZE), f32),
            pltpu.VMEM((BLK, BLK), f32),
            pltpu.VMEM((keys, HEAD_SIZE), bf16),
            pltpu.VMEM((keys, HEAD_SIZE), bf16),
            pltpu.VMEM((HEAD_SIZE, keys), bf16),
            pltpu.VMEM((keys, HEAD_SIZE), f32),
            pltpu.VMEM((keys, HEAD_SIZE), f32),
        ],
        compiler_params=pltpu.CompilerParams(vmem_limit_bytes=48 * 1024 * 1024),
        cost_estimate=pl.CostEstimate(flops=12 * 10**9, bytes_accessed=16 * 2**20, transcendentals=10**7),
        name="attention_gradients",
    )(blocks, slot, domain, ref, owner, q, r, k, v, packed_kv, packed_kv)


def enter(peers):
    barrier = pltpu.get_barrier_semaphore()
    for peer in peers:
        pl.semaphore_signal(barrier, inc=1, device_id=peer, device_id_type=pl.DeviceIdType.MESH)
    pl.semaphore_wait(barrier, len(peers))


def remote(source, target, send_sem, recv_sem, peer):
    return pltpu.make_async_remote_copy(
        src_ref=source, dst_ref=target, send_sem=send_sem, recv_sem=recv_sem,
        device_id=peer, device_id_type=pl.DeviceIdType.MESH,
    )


def gather_kernel(seq, k_ref, v_ref, out_ref, line_send, line_recv, pair_send, pair_recv):
    me, core = lax.axis_index("seq"), lax.axis_index("pair")
    width = k_ref.shape[1]
    own = me * 2 + core
    out_ref[own, :, :width] = k_ref[...]
    out_ref[own, :, width:] = v_ref[...]
    line = [{"seq": lax.rem(me + off, seq)} for off in range(1, seq)]
    partner = {"pair": 1 - core}
    enter(line + [partner])
    away, across = [], []
    for n in range(seq - 1):
        away.append(remote(out_ref.at[own], out_ref.at[own], line_send.at[n], line_recv.at[n], line[n]))
        away[n].start()
    across.append(remote(out_ref.at[own], out_ref.at[own], pair_send.at[0], pair_recv.at[0], partner))
    across[0].start()
    for n in range(seq - 1):
        away[n].wait_recv()
        held = lax.rem(me + seq - n - 1, seq) * 2 + core
        across.append(remote(out_ref.at[held], out_ref.at[held], pair_send.at[n + 1], pair_recv.at[n + 1], partner))
        across[n + 1].start()
    for copy in across:
        copy.wait()
    for copy in away:
        copy.wait_send()


def gather(k, v):
    seq = lax.axis_size("seq")
    rows, width = k.shape
    dma = pltpu.SemaphoreType.DMA
    out = pl.pallas_call(
        functools.partial(gather_kernel, seq),
        out_shape=jax.ShapeDtypeStruct((2 * seq, rows, 2 * width), k.dtype),
        in_specs=[pl.BlockSpec(memory_space=pltpu.VMEM)] * 2,
        out_specs=pl.BlockSpec(memory_space=pltpu.VMEM),
        scratch_shapes=[dma((seq,)), dma((seq,)), dma((seq,)), dma((seq,))],
        compiler_params=pltpu.CompilerParams(
            collective_id=0, has_side_effects=True, vmem_limit_bytes=24 * 1024 * 1024
        ),
        name="gather_prompt",
    )(k, v)
    return out.reshape(2 * seq * rows, 2 * width)


def scatter_kernel(
    seq, mdl, stat_ref, pk_ref, pv_ref, coef_ref, dk_ref, dv_ref,
    stat_line, stat_group, from_pair, ready, arrived,
    line_send, line_recv, group_send, group_recv, pair_send, pair_recv, out_send, out_recv,
):
    me, core, lane = lax.axis_index("seq"), lax.axis_index("pair"), lax.axis_index("mdl")
    width = pk_ref.shape[2]
    line = [{"seq": lax.rem(me + off, seq)} for off in range(1, seq)]
    spot = lane * 2 + core
    group = []
    for off in range(1, 2 * mdl):
        other = lax.rem(spot + off, 2 * mdl)
        group.append({"mdl": other // 2, "pair": lax.rem(other, 2)})
    partner = {"pair": 1 - core}
    stat_line[me] = stat_ref[...]
    stat_group[spot] = stat_ref[...]
    enter(line + group)
    small, swaps, away = [], [], []
    for n, peer in enumerate(group):
        small.append(remote(stat_ref, stat_group.at[spot], group_send.at[n], group_recv.at[n], peer))
    for n, peer in enumerate(line):
        small.append(remote(stat_ref, stat_line.at[me], line_send.at[n], line_recv.at[n], peer))
    for half, ref in enumerate((pk_ref, pv_ref)):
        for n in range(seq):
            sems = (pair_send.at[half, n], pair_recv.at[half, n])
            swaps.append(remote(ref.at[n * 2 + 1 - core], from_pair.at[half, n], *sems, partner))
    for copy in small + swaps:
        copy.start()
    for copy in small:
        copy.wait()

    def gap(side):
        total = jnp.zeros((1, BLK), jnp.float32)
        for n in range(mdl):
            total += stat_group[n * 2 + side, 0:1, :]
        return jnp.sum(total, axis=1, keepdims=True) - stat_group[side, 1:2, :]

    sign = jnp.where(core == 0, 1.0, -1.0)
    margin = dpo_beta * sign * (gap(core) - gap(1 - core))
    own_count = jnp.zeros((1, BLK), jnp.float32)
    for n in range(seq):
        own_count += jnp.where(stat_line[n, 2:3, :] == stat_ref[2:3, :], 1.0, 0.0)
    weight = seq / (NDOM * own_count)
    coef = -sign * loss_scale * weight * dpo_beta * jax.nn.sigmoid(-margin)
    coef_ref[...] = jnp.broadcast_to(coef, coef_ref.shape)
    factor = jnp.concatenate([coef] * (width // BLK), axis=1)
    for copy in swaps:
        copy.wait()
    for half, ref in enumerate((pk_ref, pv_ref)):
        for n in range(seq):
            mine = ref[n * 2 + core].astype(jnp.float32) - from_pair[half, n].astype(jnp.float32)
            ready[n, :, half * width : (half + 1) * width] = (mine * factor).astype(ready.dtype)
    for n, peer in enumerate(line):
        copy = remote(ready.at[peer["seq"]], arrived.at[me], out_send.at[n], out_recv.at[n], peer)
        copy.start()
        away.append(copy)
    total = ready[me].astype(jnp.float32)
    for n, copy in enumerate(away):
        copy.wait()
        total += arrived[lax.rem(me + seq - n - 1, seq)].astype(jnp.float32)
    dk_ref[...] = total[:, :width]
    dv_ref[...] = total[:, width:]


def scatter(stat, pk, pv, rows):
    seq, mdl = lax.axis_size("seq"), lax.axis_size("mdl")
    width = pk.shape[1]
    f32, bf16, dma = jnp.float32, pk.dtype, pltpu.SemaphoreType.DMA
    vmem = pl.BlockSpec(memory_space=pltpu.VMEM)
    return pl.pallas_call(
        functools.partial(scatter_kernel, seq, mdl),
        out_shape=[
            jax.ShapeDtypeStruct((8, BLK), f32),
            jax.ShapeDtypeStruct((rows, width), f32),
            jax.ShapeDtypeStruct((rows, width), f32),
        ],
        in_specs=[vmem] * 3,
        out_specs=[vmem] * 3,
        scratch_shapes=[
            pltpu.VMEM((seq, 8, BLK), f32),
            pltpu.VMEM((2 * mdl, 8, BLK), f32),
            pltpu.VMEM((2, seq, rows, width), bf16),
            pltpu.VMEM((seq, rows, 2 * width), bf16),
            pltpu.VMEM((seq, rows, 2 * width), bf16),
            dma((seq,)), dma((seq,)), dma((2 * mdl,)), dma((2 * mdl,)),
            dma((2, seq)), dma((2, seq)), dma((seq,)), dma((seq,)),
        ],
        compiler_params=pltpu.CompilerParams(
            collective_id=1, has_side_effects=True, vmem_limit_bytes=24 * 1024 * 1024
        ),
        name="scatter_prompt_gradients",
    )(stat, pk.reshape(2 * seq, rows, width), pv.reshape(2 * seq, rows, width))


def per_device(
    resp_query, resp_key, response_value, readout, packed_prompt_key, packed_prompt_value,
    prompt_owner, pair_slot, domain_of, resp_blocks, ref_logprob,
):
    packed_kv = gather(packed_prompt_key, packed_prompt_value)
    dq, dk, dv, pk, pv, stat = attention(
        resp_query, readout, resp_key, response_value, packed_kv,
        prompt_owner[None, :], pair_slot, resp_blocks, domain_of, ref_logprob,
    )
    coef, key_prompt, value_prompt = scatter(stat, pk, pv, packed_prompt_key.shape[0])

    def scaled(array):
        return (array.astype(jnp.float32) * coef[0, 0]).astype(jnp.bfloat16)

    return scaled(dq), scaled(dk), scaled(dv), key_prompt, value_prompt


def solution(mesh):
    tokens = P(("grp", "seq", "pair"), "mdl")
    each = P(("grp", "seq", "pair"))
    in_specs = (tokens,) * 6 + (P("grp"), P(("grp", "seq")), P(("grp", "seq")), each, each)
    return jax.shard_map(per_device, mesh=mesh, in_specs=in_specs, out_specs=(tokens,) * 5, check_vma=False)
```

```python
import functools
import math

import jax
import jax.numpy as jnp
from jax import lax
from jax.experimental import pallas as pl
from jax.experimental.pallas import tpu as pltpu
from jax.sharding import PartitionSpec as P

HEAD_SIZE = 128
PROMPT_DEV = 64
BLK = 128
NDOM = 8
WINDOW = 4 * PROMPT_DEV
NEG = -1e30
VMEM_BYTES = 60 * 2**20
AT_ONCE = 2

dpo_beta = 0.5
loss_scale = 256.0


def dot(left, right, left_dim, right_dim):
    return lax.dot_general(
        left, right, (((left_dim,), (right_dim,)), ((), ())), preferred_element_type=jnp.float32
    )


def open_chain(rb, heads, q_ref, r_ref, kcat, vcat):
    seen = WINDOW + BLK * (rb + 1)
    rows = slice(rb * BLK, (rb + 1) * BLK)
    queries = jnp.concatenate([q_ref[rows, h * HEAD_SIZE : (h + 1) * HEAD_SIZE] for h in heads], axis=0)
    reads = jnp.concatenate([r_ref[rows, h * HEAD_SIZE : (h + 1) * HEAD_SIZE] for h in heads], axis=0)
    return queries, reads, dot(kcat[:seen, :], queries, 1, 1), dot(vcat[:seen, :], reads, 1, 1)


def weigh_chain(rb, heads, state, blocks, bias, tri):
    queries, reads, scores, dprob = state
    log_scale = HEAD_SIZE**-0.5 * math.log2(math.e)
    seen = WINDOW + BLK * (rb + 1)
    wide = len(heads)
    parts = [scores[:WINDOW] + jnp.concatenate([bias[...]] * wide, axis=1)]
    if rb:
        parts.append(scores[WINDOW : seen - BLK])
    parts.append(scores[seen - BLK :] + jnp.concatenate([tri[...]] * wide, axis=1))
    scores = jnp.concatenate(parts, axis=0)
    top = jnp.max(scores, axis=0, keepdims=True) * log_scale
    exponent = jnp.exp2(scores * log_scale - top)
    inverse = jnp.where(rb < blocks, 1.0, 0.0) / jnp.sum(exponent, axis=0, keepdims=True)
    row_dot = jnp.sum(exponent * dprob, axis=0, keepdims=True) * inverse
    weights = exponent * inverse
    dscore = (weights * (dprob - row_dot)).astype(jnp.bfloat16)
    return queries, reads, weights.astype(jnp.bfloat16), dscore, row_dot


def close_chain(rb, heads, state, dq_ref, lp_ref, kt, dkacc, dvacc):
    queries, reads, weights, dscore, row_dot = state
    seen = WINDOW + BLK * (rb + 1)
    rows = slice(rb * BLK, (rb + 1) * BLK)
    dvacc[:seen, :] += dot(weights, reads, 1, 0)
    dkacc[:seen, :] += dot(dscore, queries, 1, 0)
    dq = (dot(kt[:, :seen], dscore, 1, 0) * HEAD_SIZE**-0.5).T.astype(jnp.bfloat16)
    for n, h in enumerate(heads):
        dq_ref[rows, h * HEAD_SIZE : (h + 1) * HEAD_SIZE] = dq[n * BLK : (n + 1) * BLK]
        lp_ref[0:1, :] += row_dot[:, n * BLK : (n + 1) * BLK]


def run_chains(chains, blocks, q_ref, r_ref, dq_ref, lp_ref, kcat, vcat, kt, bias, tri, dkacc, dvacc):
    opened = open_chain(*chains[0], q_ref, r_ref, kcat, vcat)
    weighed = None
    for n, chain in enumerate(chains):
        following = open_chain(*chains[n + 1], q_ref, r_ref, kcat, vcat) if n + 1 < len(chains) else None
        done = weigh_chain(*chain, opened, blocks, bias, tri)
        if weighed is not None:
            close_chain(*chains[n - 1], weighed, dq_ref, lp_ref, kt, dkacc, dvacc)
        opened, weighed = following, done
    close_chain(*chains[-1], weighed, dq_ref, lp_ref, kt, dkacc, dvacc)


def attention_kernel(
    group, at_once, blocks_ref, slot_ref, domain_ref, ref_ref, owner_ref, q_ref, r_ref, k_ref, v_ref, gk_ref, gv_ref,
    dq_ref, dk_ref, dv_ref, pk_ref, pv_ref, lp_ref,
    sel, bias, tri, kcat, vcat, kt, dkacc, dvacc,
):
    @pl.when(pl.program_id(0) == 0)
    def _():
        owner = owner_ref[...]
        slot = slot_ref[0]
        first = jnp.sum(jnp.where(owner < slot, 1.0, 0.0), axis=1, keepdims=True).astype(jnp.int32)
        column = lax.broadcasted_iota(jnp.int32, sel.shape, 1)
        row = lax.broadcasted_iota(jnp.int32, sel.shape, 0)
        chosen = jnp.where((column - row == first) & (owner == slot), 1.0, 0.0)
        sel[...] = chosen.astype(jnp.bfloat16)
        shown = jnp.sum(chosen, axis=1, keepdims=True)
        bias[...] = jnp.broadcast_to(jnp.where(shown > 0.5, 0.0, NEG), bias.shape)
        key = lax.broadcasted_iota(jnp.int32, tri.shape, 0)
        query = lax.broadcasted_iota(jnp.int32, tri.shape, 1)
        tri[...] = jnp.where(key > query, NEG, 0.0)
        line = lax.broadcasted_iota(jnp.int32, lp_ref.shape, 0)
        domain = jnp.full(lp_ref.shape, domain_ref[0], jnp.int32).astype(jnp.float32)
        lp_ref[...] = jnp.where(line == 1, ref_ref[0], jnp.where(line == 2, domain, 0.0))

    kcat[:WINDOW, :] = dot(sel[...], gk_ref[...], 1, 0).astype(jnp.bfloat16)
    vcat[:WINDOW, :] = dot(sel[...], gv_ref[...], 1, 0).astype(jnp.bfloat16)
    kcat[WINDOW:, :] = k_ref[...]
    vcat[WINDOW:, :] = v_ref[...]
    kt[...] = kcat[...].T
    dkacc[...] = jnp.zeros_like(dkacc)
    dvacc[...] = jnp.zeros_like(dvacc)
    chains = [(rb, tuple(range(start, start + at_once))) for rb in range(q_ref.shape[0] // BLK) for start in range(0, group, at_once)]
    run_chains(chains, blocks_ref[0], q_ref, r_ref, dq_ref, lp_ref, kcat, vcat, kt, bias, tri, dkacc, dvacc)
    scale = HEAD_SIZE**-0.5
    dk_ref[...] = (dkacc[WINDOW:, :] * scale).astype(dk_ref.dtype)
    dv_ref[...] = dvacc[WINDOW:, :].astype(dv_ref.dtype)
    pk_ref[...] = dot(sel[...], (dkacc[:WINDOW, :] * scale).astype(jnp.bfloat16), 0, 0).astype(pk_ref.dtype)
    pv_ref[...] = dot(sel[...], dvacc[:WINDOW, :].astype(jnp.bfloat16), 0, 0).astype(pv_ref.dtype)


def attention(q, r, k, v, packed_kv, owner, slot, blocks, domain, ref):
    rows, columns = q.shape
    tokens = packed_kv.shape[0]
    heads = k.shape[1] // HEAD_SIZE
    group = columns // k.shape[1]
    wide = pl.BlockSpec((rows, group * HEAD_SIZE), lambda g: (0, g))
    slim = pl.BlockSpec((rows, HEAD_SIZE), lambda g: (0, g))
    packed = pl.BlockSpec((tokens, HEAD_SIZE), lambda g: (0, g))
    packed_value = pl.BlockSpec((tokens, HEAD_SIZE), lambda g: (0, heads + g))
    smem = pl.BlockSpec(memory_space=pltpu.SMEM)
    keys = WINDOW + rows
    bf16, f32 = jnp.bfloat16, jnp.float32
    return pl.pallas_call(
        functools.partial(attention_kernel, group, AT_ONCE),
        grid=(heads,),
        in_specs=[smem] * 4
        + [pl.BlockSpec((1, tokens), lambda g: (0, 0)), wide, wide, slim, slim, packed, packed_value],
        out_specs=[wide, slim, slim, packed, packed, pl.BlockSpec((8, BLK), lambda g: (0, 0))],
        out_shape=[
            jax.ShapeDtypeStruct((rows, columns), bf16),
            jax.ShapeDtypeStruct(k.shape, bf16),
            jax.ShapeDtypeStruct(k.shape, bf16),
            jax.ShapeDtypeStruct((tokens, k.shape[1]), bf16),
            jax.ShapeDtypeStruct((tokens, k.shape[1]), bf16),
            jax.ShapeDtypeStruct((8, BLK), f32),
        ],
        scratch_shapes=[
            pltpu.VMEM((WINDOW, tokens), bf16),
            pltpu.VMEM((WINDOW, HEAD_SIZE), f32),
            pltpu.VMEM((BLK, BLK), f32),
            pltpu.VMEM((keys, HEAD_SIZE), bf16),
            pltpu.VMEM((keys, HEAD_SIZE), bf16),
            pltpu.VMEM((HEAD_SIZE, keys), bf16),
            pltpu.VMEM((keys, HEAD_SIZE), f32),
            pltpu.VMEM((keys, HEAD_SIZE), f32),
        ],
        compiler_params=pltpu.CompilerParams(vmem_limit_bytes=VMEM_BYTES),
        cost_estimate=pl.CostEstimate(flops=12 * 10**9, bytes_accessed=16 * 2**20, transcendentals=10**7),
        name="attention_gradients",
    )(blocks, slot, domain, ref, owner, q, r, k, v, packed_kv, packed_kv)


def enter(peers):
    barrier = pltpu.get_barrier_semaphore()
    for peer in peers:
        pl.semaphore_signal(barrier, inc=1, device_id=peer, device_id_type=pl.DeviceIdType.MESH)
    pl.semaphore_wait(barrier, len(peers))


def remote(source, target, send_sem, recv_sem, peer):
    return pltpu.make_async_remote_copy(
        src_ref=source, dst_ref=target, send_sem=send_sem, recv_sem=recv_sem,
        device_id=peer, device_id_type=pl.DeviceIdType.MESH,
    )


def gather_kernel(seq, k_ref, v_ref, out_ref, line_send, line_recv, pair_send, pair_recv):
    me, core = lax.axis_index("seq"), lax.axis_index("pair")
    width = k_ref.shape[1]
    own = me * 2 + core
    out_ref[own, :, :width] = k_ref[...]
    out_ref[own, :, width:] = v_ref[...]
    line = [{"seq": lax.rem(me + off, seq)} for off in range(1, seq)]
    partner = {"pair": 1 - core}
    enter(line + [partner])
    away, across = [], []
    for n in range(seq - 1):
        away.append(remote(out_ref.at[own], out_ref.at[own], line_send.at[n], line_recv.at[n], line[n]))
        away[n].start()
    across.append(remote(out_ref.at[own], out_ref.at[own], pair_send.at[0], pair_recv.at[0], partner))
    across[0].start()
    for n in range(seq - 1):
        away[n].wait_recv()
        held = lax.rem(me + seq - n - 1, seq) * 2 + core
        across.append(remote(out_ref.at[held], out_ref.at[held], pair_send.at[n + 1], pair_recv.at[n + 1], partner))
        across[n + 1].start()
    for copy in across:
        copy.wait()
    for copy in away:
        copy.wait_send()


def gather(k, v):
    seq = lax.axis_size("seq")
    rows, width = k.shape
    dma = pltpu.SemaphoreType.DMA
    out = pl.pallas_call(
        functools.partial(gather_kernel, seq),
        out_shape=jax.ShapeDtypeStruct((2 * seq, rows, 2 * width), k.dtype),
        in_specs=[pl.BlockSpec(memory_space=pltpu.VMEM)] * 2,
        out_specs=pl.BlockSpec(memory_space=pltpu.VMEM),
        scratch_shapes=[dma((seq,)), dma((seq,)), dma((seq,)), dma((seq,))],
        compiler_params=pltpu.CompilerParams(
            collective_id=0, has_side_effects=True, vmem_limit_bytes=VMEM_BYTES
        ),
        name="gather_prompt",
    )(k, v)
    return out.reshape(2 * seq * rows, 2 * width)


def scatter_kernel(
    seq, mdl, stat_ref, pk_ref, pv_ref, gq_ref, gk_ref, gv_ref, dk_ref, dv_ref, oq_ref, ok_ref, ov_ref,
    held, load_sem, store_sem, stat_line, stat_group, from_pair, ready, arrived,
    line_send, line_recv, group_send, group_recv, pair_send, pair_recv, out_send, out_recv,
):
    me, core, lane = lax.axis_index("seq"), lax.axis_index("pair"), lax.axis_index("mdl")
    width = pk_ref.shape[2]
    line = [{"seq": lax.rem(me + off, seq)} for off in range(1, seq)]
    spot = lane * 2 + core
    group = []
    for off in range(1, 2 * mdl):
        other = lax.rem(spot + off, 2 * mdl)
        group.append({"mdl": other // 2, "pair": lax.rem(other, 2)})
    partner = {"pair": 1 - core}
    parts = [pl.ds(start, BLK) for start in range(0, held.shape[0], BLK)]
    loads = [pltpu.make_async_copy(gq_ref.at[p], held.at[p], load_sem.at[n]) for n, p in enumerate(parts)]
    stores = [pltpu.make_async_copy(held.at[p], oq_ref.at[p], store_sem.at[n]) for n, p in enumerate(parts)]
    for copy in loads:
        copy.start()
    stat_line[me] = stat_ref[...]
    stat_group[spot] = stat_ref[...]
    enter(line + group)
    small, swaps, away = [], [], []
    for n, peer in enumerate(group):
        small.append(remote(stat_ref, stat_group.at[spot], group_send.at[n], group_recv.at[n], peer))
    for n, peer in enumerate(line):
        small.append(remote(stat_ref, stat_line.at[me], line_send.at[n], line_recv.at[n], peer))
    for half, ref in enumerate((pk_ref, pv_ref)):
        for n in range(seq):
            sems = (pair_send.at[half, n], pair_recv.at[half, n])
            swaps.append(remote(ref.at[n * 2 + 1 - core], from_pair.at[half, n], *sems, partner))
    for copy in small + swaps:
        copy.start()
    for copy in small:
        copy.wait()

    def gap(side):
        total = jnp.zeros((1, BLK), jnp.float32)
        for n in range(mdl):
            total += stat_group[n * 2 + side, 0:1, :]
        return jnp.sum(total, axis=1, keepdims=True) - stat_group[side, 1:2, :]

    sign = jnp.where(core == 0, 1.0, -1.0)
    margin = dpo_beta * sign * (gap(core) - gap(1 - core))
    own_count = jnp.zeros((1, BLK), jnp.float32)
    for n in range(seq):
        own_count += jnp.where(stat_line[n, 2:3, :] == stat_ref[2:3, :], 1.0, 0.0)
    weight = seq / (NDOM * own_count)
    coef = -sign * loss_scale * weight * dpo_beta * jax.nn.sigmoid(-margin)
    factor = jnp.concatenate([coef] * (width // BLK), axis=1)
    for copy in swaps:
        copy.wait()
    for half, ref in enumerate((pk_ref, pv_ref)):
        for n in range(seq):
            mine = ref[n * 2 + core].astype(jnp.float32) - from_pair[half, n].astype(jnp.float32)
            ready[n, :, half * width : (half + 1) * width] = (mine * factor).astype(ready.dtype)
    for n, peer in enumerate(line):
        copy = remote(ready.at[peer["seq"]], arrived.at[me], out_send.at[n], out_recv.at[n], peer)
        copy.start()
        away.append(copy)
    wide = jnp.concatenate([coef] * (held.shape[1] // BLK), axis=1)
    for n, p in enumerate(parts):
        loads[n].wait()
        held[p] = (held[p].astype(jnp.float32) * wide).astype(held.dtype)
        stores[n].start()
    ok_ref[...] = (gk_ref[...].astype(jnp.float32) * factor).astype(ok_ref.dtype)
    ov_ref[...] = (gv_ref[...].astype(jnp.float32) * factor).astype(ov_ref.dtype)
    total = ready[me].astype(jnp.float32)
    for n, copy in enumerate(away):
        copy.wait()
        total += arrived[lax.rem(me + seq - n - 1, seq)].astype(jnp.float32)
    dk_ref[...] = total[:, :width]
    dv_ref[...] = total[:, width:]
    for copy in stores:
        copy.wait()


def scatter(stat, pk, pv, dq, dk, dv, rows):
    seq, mdl = lax.axis_size("seq"), lax.axis_size("mdl")
    width = pk.shape[1]
    f32, bf16, dma = jnp.float32, pk.dtype, pltpu.SemaphoreType.DMA
    vmem = pl.BlockSpec(memory_space=pltpu.VMEM)
    whole = pl.BlockSpec(memory_space=pl.ANY)
    return pl.pallas_call(
        functools.partial(scatter_kernel, seq, mdl),
        out_shape=[
            jax.ShapeDtypeStruct((rows, width), f32),
            jax.ShapeDtypeStruct((rows, width), f32),
            jax.ShapeDtypeStruct(dq.shape, dq.dtype),
            jax.ShapeDtypeStruct(dk.shape, dk.dtype),
            jax.ShapeDtypeStruct(dv.shape, dv.dtype),
        ],
        in_specs=[vmem] * 3 + [whole, vmem, vmem],
        out_specs=[vmem] * 2 + [whole, vmem, vmem],
        scratch_shapes=[
            pltpu.VMEM(dq.shape, dq.dtype),
            dma((dq.shape[0] // BLK,)), dma((dq.shape[0] // BLK,)),
            pltpu.VMEM((seq, 8, BLK), f32),
            pltpu.VMEM((2 * mdl, 8, BLK), f32),
            pltpu.VMEM((2, seq, rows, width), bf16),
            pltpu.VMEM((seq, rows, 2 * width), bf16),
            pltpu.VMEM((seq, rows, 2 * width), bf16),
            dma((seq,)), dma((seq,)), dma((2 * mdl,)), dma((2 * mdl,)),
            dma((2, seq)), dma((2, seq)), dma((seq,)), dma((seq,)),
        ],
        compiler_params=pltpu.CompilerParams(
            collective_id=1, has_side_effects=True, vmem_limit_bytes=VMEM_BYTES
        ),
        name="scatter_prompt_gradients",
    )(stat, pk.reshape(2 * seq, rows, width), pv.reshape(2 * seq, rows, width), dq, dk, dv)


def per_device(
    resp_query, resp_key, response_value, readout, packed_prompt_key, packed_prompt_value,
    prompt_owner, pair_slot, domain_of, resp_blocks, ref_logprob,
):
    packed_kv = gather(packed_prompt_key, packed_prompt_value)
    dq, dk, dv, pk, pv, stat = attention(
        resp_query, readout, resp_key, response_value, packed_kv,
        prompt_owner[None, :], pair_slot, resp_blocks, domain_of, ref_logprob,
    )
    key_prompt, value_prompt, dq, dk, dv = scatter(stat, pk, pv, dq, dk, dv, packed_prompt_key.shape[0])
    return dq, dk, dv, key_prompt, value_prompt


def solution(mesh):
    tokens = P(("grp", "seq", "pair"), "mdl")
    each = P(("grp", "seq", "pair"))
    in_specs = (tokens,) * 6 + (P("grp"), P(("grp", "seq")), P(("grp", "seq")), each, each)
    return jax.shard_map(per_device, mesh=mesh, in_specs=in_specs, out_specs=(tokens,) * 5, check_vma=False)
```
